128 devices in a mesh: gx: 8 (over x, core), gz: 16 (over y, z).
Axes of the slice: x: 4, y: 4, z: 4, core: 2. Of those that a mesh axis runs over, the one named last changes fastest.
Arguments:
- velocity: float32 [3, 256, 512, 256], P(None, 'gz', 'gx'), may hold values from -6 to 6
- mean_flow: float32 [256], replicated, may hold values from 0.2 to 1
- fibres: float32 [6, 524288], P(None, ('gx', 'gz')), may hold values from -0.6 to 0.6
- moves: int32 [524288, 1], P(('gx', 'gz')), may hold values from 0 to 8, as said below
- grad_rows: int32 [24576], P(('gx', 'gz')), may hold values from 0 to 2047
- grad_readers: int32 [24576, 1], P(('gx', 'gz')), may hold values from 0 to 127; in each aligned block of 192 rows (0 to 191, 192 to 383, ...) at most 2 rows name the same one
- fibre_cell: int32 [655360], P(('gx', 'gz')), may hold values from 0 to 32767
Outputs:
- advanced_flow: float32 [3, 256, 512, 256], P(None, 'gz', 'gx')
- fibres_out: float32 [6, 655360], P(None, ('gx', 'gz'))
The draws below stay inside these ranges and needn't reach their ends.
Inputs may be any that keep to these rules, and one draw needn't show every extreme that they name: `moves`: of one device's fibres at most 128 take any one code other than 4, and on every device some code other than 4 is taken by exactly 128; all other fibres have code 4. `grad_readers`: of one device's list entries at most 2 name the same reader, a bound that some block reaches.
All inputs are finite; a program needn't handle non-finite values.
Results may differ from the reference program's by a relative error of at most 0.0003.
Values sent between devices are 32-bit elements; how exact they have to be, the bound alone decides.
A program may use at most 128 MiB of HBM per device.

```python
import math
import jax
import jax.numpy as jnp
import numpy as np

CX = 64
CZ = 16
NY = 256
SUB = 2
REC = 6
FIB_DEV = 4096
CAP = 128
SLOT_DEV = 5120
RCAP = 2
GR_DEV = 192
ROWS_DEV = 2048
NX = 512
NZ = 256
FIBRES = 524288
SLOTS = 655360
LIST = 24576
N_GX = 8
N_GZ = 16


def block_codes(block_key):
    count_key = jax.random.fold_in(block_key, 11)
    pick_key = jax.random.fold_in(block_key, 12)
    order_key = jax.random.fold_in(block_key, 13)
    counts = jax.random.randint(count_key, (8,), CAP // 4, CAP + 1)
    chosen = jax.random.randint(pick_key, (), 0, 8)
    counts = jnp.where(jnp.arange(8, dtype=jnp.int32) == chosen, CAP, counts).astype(jnp.int32)
    bounds = jnp.cumsum(counts).astype(jnp.int32)
    ranks = jax.random.permutation(order_key, FIB_DEV).astype(jnp.int32)
    mover = jnp.sum((ranks[:, None] >= bounds[None, :]).astype(jnp.int32), axis=1)
    return jnp.where(mover == 8, 4, jnp.where(mover < 4, mover, mover + 1)).astype(jnp.int32)


def draw_moves(key, part):
    key = jax.random.fold_in(key, 1)
    blocks = FIBRES // FIB_DEV
    keys = jax.vmap(lambda b: jax.random.fold_in(key, b))(jnp.arange(blocks, dtype=jnp.int32))
    codes = jax.vmap(block_codes)(keys)
    return codes.reshape(FIBRES, 1)


def set_ends(values, rng, smallest, largest):
    longest = values.shape.index(max(values.shape))
    spots = []
    for shift in (0, 1):
        where = [jax.random.randint(jax.random.fold_in(rng, axis), (), 0, length) for axis, length in enumerate(values.shape)]
        where[longest] = (where[longest] + shift) % values.shape[longest]
        spots.append(tuple(where))
    return values.at[spots[0]].set(smallest).at[spots[1]].set(largest)


def block_levels(own_key, shape, shards, low, largest):
    def one(dim, blocks):
        steps = jax.random.uniform(jax.random.fold_in(jax.random.fold_in(own_key, 6), dim), (blocks,), jnp.float32, low / len(shards), largest / len(shards))
        return jnp.repeat(jnp.exp(steps), shape[dim] // blocks).reshape((-1,) + (1,) * (len(shape) - dim - 1))

    loudness = one(*shards[0])
    for cut in shards[1:]:
        loudness = loudness * one(*cut)
    return loudness


def assign_block(key, own, number, rows, number_of, top, bound, lean):
    sequence = jax.random.permutation(key, number_of)
    heavy_load, ordinary = load_shares(number_of, rows * top, bound, lean, True), load_shares(number_of, rows * top, bound, lean, False)
    places = jnp.arange(number_of)

    def named(lengths, turn):
        used = int((lengths > 0).sum())
        fixed = max(1, used // 4)
        shifted = fixed + (places - fixed + turn * (used - fixed)) % max(1, number_of - fixed)
        return jnp.zeros((number_of,), jnp.int32).at[sequence[jnp.where(places < fixed, places, shifted)]].set(jnp.asarray(lengths, jnp.int32))

    lengths = jnp.where(number % 4 == 0, named(heavy_load, number // 4), named(ordinary, number - number // 4 - 1))
    mixed = jax.random.permutation(jax.random.fold_in(own, 3), number_of)
    donor, receiver = mixed[0:number_of // 2 * 2:2], mixed[1:number_of // 2 * 2:2]
    margin = jnp.minimum(lengths[donor] - 1, bound - lengths[receiver]) // 2
    margin = jnp.where((donor == sequence[0]) | (receiver == sequence[0]) | (lengths[receiver] == 0), 0, jnp.maximum(margin, 0))
    shifted = jax.random.randint(jax.random.fold_in(own, 4), (number_of // 2,), 0, 1 << 20) % (margin + 1)
    lengths = lengths.at[donor].add(-shifted).at[receiver].add(shifted)
    items = jnp.searchsorted(jnp.cumsum(lengths), jnp.arange(rows * top), side="right").astype(jnp.int32)
    grid = items.reshape(top, rows).T
    grid = grid[jax.random.permutation(jax.random.fold_in(own, 1), rows)]
    turn = jax.random.randint(jax.random.fold_in(own, 2), (rows, 1), 0, top)
    return jnp.take_along_axis(grid, (jnp.arange(top)[None, :] + turn) % top, axis=1)


def load_shares(number_of, total, limit, slope, full):
    weights = [(1 << 20) // math.isqrt(standing ** slope) + 1 for standing in range(1, number_of + 1)]
    largest = limit if full else min(limit, max(-(-total // number_of), total * weights[0] // sum(weights)))
    least = 1 if total - largest >= number_of - 1 else 0
    given, spare = [largest] + [least] * (number_of - 1), total - largest - least * (number_of - 1)
    while spare > 0:
        movable = [i for i in range(1, number_of) if given[i] < largest] or [i for i in range(1, number_of) if given[i] < limit]
        whole, remaining = sum([weights[i] for i in movable]), spare
        for i in movable:
            more = min(limit - given[i], max(1, remaining * weights[i] // whole), spare)
            given[i] = given[i] + more
            spare = spare - more
    return np.array(given)


def noise(key, shape, scale, reach, shards=(), kind=jnp.bfloat16):
    values = jax.random.normal(key, shape, jnp.float32) * scale
    if len(shards) > 0:
        values = block_levels(key, shape, shards, -0.22, 0.18) * values
    return jnp.clip(values, min=-reach, max=reach).astype(kind)


def setup_inputs(seed: int = 0) -> dict:
    streams_of = jax.random.split(jax.random.key(seed), 8)
    velocity = noise(streams_of[0], (3, NZ, NX, NY), 1.0, 6.0, ((1, 16), (2, 8)), jnp.float32)
    mean_flow = jnp.clip(jax.random.uniform(streams_of[1], (NY,), jnp.float32, 0.2, 1.0), 0.2, 1.0)
    fibres = jnp.clip(jax.random.uniform(streams_of[2], (REC, FIBRES), jnp.float32, -0.6, 0.6) * block_levels(streams_of[2], (REC, FIBRES), ((1, 128),), -0.4, 0.0), -0.6, 0.6)
    moves = draw_moves(jax.random.fold_in(streams_of[7], 71), 0)
    grad_rows = set_ends(jax.random.randint(streams_of[4], (LIST,), 0, ROWS_DEV), jax.random.fold_in(streams_of[4], 1), 0, ROWS_DEV - 1).astype(jnp.int32)
    grad_readers_keys = jax.random.split(jax.random.fold_in(streams_of[5], 1), LIST // GR_DEV)
    grad_readers_turns = jax.random.permutation(jax.random.fold_in(streams_of[5], 3), LIST // GR_DEV)
    grad_readers = jax.vmap(lambda own, number: assign_block(jax.random.fold_in(streams_of[5], 2), own, number, GR_DEV, N_GX * N_GZ, 1, RCAP, 2))(grad_readers_keys, grad_readers_turns).reshape((LIST, 1))
    fibre_cell = set_ends(jax.random.randint(streams_of[6], (SLOTS,), 0, N_GX * N_GZ * RCAP * 128), jax.random.fold_in(streams_of[6], 1), 0, (N_GX * N_GZ * RCAP * 128) - 1).astype(jnp.int32)
    return dict(velocity=velocity, mean_flow=mean_flow, fibres=fibres, moves=moves, grad_rows=grad_rows, grad_readers=grad_readers, fibre_cell=fibre_cell)


DIFFUSION = 0.1
ADVECTION = 0.4
SHAPE_FACTOR = 0.9
TURN_STEP = 0.25


def update(padded, mean_flow):
    centre = padded[:, 1:-1, 1:-1, 1:-1]
    beside_all = padded[:, 2:, 1:-1, 1:-1] + padded[:, :-2, 1:-1, 1:-1]
    beside_all = beside_all + padded[:, 1:-1, 2:, 1:-1] + padded[:, 1:-1, :-2, 1:-1]
    beside_all = beside_all + padded[:, 1:-1, 1:-1, 2:] + padded[:, 1:-1, 1:-1, :-2]
    streamwise = 0.5 * (padded[:, 1:-1, 2:, 1:-1] - padded[:, 1:-1, :-2, 1:-1])
    return centre + DIFFUSION * (beside_all - 6.0 * centre) - ADVECTION * mean_flow * streamwise


def gradient(padded):
    along_x = 0.5 * (padded[:, 1:-1, 2:, 1:-1] - padded[:, 1:-1, :-2, 1:-1])
    along_y = 0.5 * (padded[:, 1:-1, 1:-1, 2:] - padded[:, 1:-1, 1:-1, :-2])
    along_z = 0.5 * (padded[:, 2:, 1:-1, 1:-1] - padded[:, :-2, 1:-1, 1:-1])
    return jnp.stack([along_x, along_y, along_z], axis=1)


def extend_whole(flow_field):
    padded = jnp.pad(flow_field, ((0, 0), (1, 1), (1, 1), (0, 0)), mode="wrap")
    return jnp.pad(padded, ((0, 0), (0, 0), (0, 0), (1, 1)))


def pack_rows(row_table, wanted, readers, devices):
    onehot = (readers[:, None] == jnp.arange(devices, dtype=jnp.int32)[None, :]).astype(jnp.int32)
    slot_rank = jnp.sum((jnp.cumsum(onehot, axis=0) - onehot) * onehot, axis=1)
    slot_pos = readers * RCAP + slot_rank
    return jnp.zeros((devices * RCAP, row_table.shape[1]), jnp.float32).at[slot_pos].set(row_table[wanted])


def code_offset(code):
    return code * CAP if code <= 4 else FIB_DEV + (code - 1) * CAP


def code_width(code):
    return FIB_DEV if code == 4 else CAP


def pack_fibres(records, move_code):
    onehot = (move_code[:, None] == jnp.arange(9, dtype=jnp.int32)[None, :]).astype(jnp.int32)
    slot_rank = jnp.sum((jnp.cumsum(onehot, axis=0) - onehot) * onehot, axis=1)
    offset = jnp.where(move_code <= 4, move_code * CAP, FIB_DEV + (move_code - 1) * CAP)
    slot_pos = offset + slot_rank
    return jnp.zeros((records.shape[0], SLOT_DEV), jnp.float32).at[:, slot_pos].set(records)


def jeffery(records, tensor):
    orient = records[3:6]
    along = jnp.stack([tensor[3 * comp] * orient[0] + tensor[3 * comp + 1] * orient[1] + tensor[3 * comp + 2] * orient[2] for comp in range(3)])
    across = jnp.stack([tensor[comp] * orient[0] + tensor[3 + comp] * orient[1] + tensor[6 + comp] * orient[2] for comp in range(3)])
    strain = 0.5 * (along + across)
    rotation = 0.5 * (along - across)
    stretch = orient[0] * along[0] + orient[1] * along[1] + orient[2] * along[2]
    turned = orient + TURN_STEP * (rotation + SHAPE_FACTOR * (strain - stretch * orient))
    return jnp.concatenate([records[0:3], turned], axis=0)


def reference(velocity, mean_flow, fibres, moves, grad_rows, grad_readers, fibre_cell):
    devices = N_GX * N_GZ
    flow_field = velocity
    for substep in range(SUB):
        flow_field = update(extend_whole(flow_field), mean_flow)
    grads = gradient(extend_whole(flow_field)).reshape(9, N_GZ, CZ, N_GX, CX, NY // 128, 128)
    row_table = grads.transpose(3, 1, 2, 4, 5, 0, 6).reshape(devices, ROWS_DEV, 9 * 128)
    send_rows = jax.vmap(lambda tab, want, read: pack_rows(tab, want, read, devices))(
        row_table, grad_rows.reshape(devices, GR_DEV), grad_readers[:, 0].reshape(devices, GR_DEV))
    received = send_rows.reshape(devices, devices, RCAP, 9 * 128).transpose(1, 0, 2, 3)
    received = received.reshape(devices, devices * RCAP, 9, 128).transpose(0, 2, 1, 3).reshape(devices, 9, devices * RCAP * 128)
    records = fibres.reshape(REC, devices, FIB_DEV).transpose(1, 0, 2)
    sending = jax.vmap(pack_fibres)(records, moves[:, 0].reshape(devices, FIB_DEV))
    sending = sending.reshape(N_GX, N_GZ, REC, SLOT_DEV)
    pieces = []
    for code in range(9):
        start = code_offset(code)
        piece = sending[:, :, :, start:start + code_width(code)]
        pieces.append(jnp.roll(piece, (code // 3 - 1, code % 3 - 1), axis=(0, 1)))
    arrived = jnp.concatenate(pieces, axis=3).reshape(devices, REC, SLOT_DEV)
    cell_index = fibre_cell.reshape(devices, SLOT_DEV)
    tensors = jax.vmap(lambda flat, idx: jnp.take(flat, idx, axis=1))(received, cell_index)
    result = jax.vmap(jeffery)(arrived, tensors)
    return flow_field, result.transpose(1, 0, 2).reshape(REC, devices * SLOT_DEV)
```

```python
import functools

import jax
import jax.numpy as jnp
from jax import lax
from jax.experimental import pallas as pl
from jax.experimental.pallas import tpu as pltpu
from jax.sharding import PartitionSpec as P

FIB_DEV = 4096
CAP = 128
SLOT_DEV = 5120
RCAP = 2
CX, CZ, NY = 64, 16, 256
XW = 72
ROWS = 2048

DIFFUSION = 0.1
ADVECTION = 0.4
SHAPE_FACTOR = 0.9
TURN_STEP = 0.25

MESH = pl.DeviceIdType.MESH
F32 = jnp.float32
BF16 = jnp.bfloat16
I32 = jnp.int32
MIB = 2**20


def code_offset(code):
    return code * CAP if code <= 4 else FIB_DEV + (code - 1) * CAP


def place(device, gz_size):
    return (device // gz_size, lax.rem(device, gz_size))


def split3(x):
    hi = x.astype(BF16).astype(F32)
    mid = (x - hi).astype(BF16).astype(F32)
    return hi, mid, x - hi - mid


def iota(shape, dim):
    return lax.broadcasted_iota(I32, shape, dim)


def slot_list(rows_ref, readers_ref):
    n = rows_ref.shape[1]
    rows, readers = rows_ref[...], readers_ref[...]
    sub, lane = iota((n, n), 0), iota((n, n), 1)
    diag = sub == lane

    def column(row):
        return jnp.sum(jnp.where(diag, jnp.broadcast_to(row, (n, n)), 0), axis=1, keepdims=True)

    same = (column(readers) == readers) & (sub < lane)
    rank = jnp.sum(same.astype(I32), axis=0, keepdims=True)
    slot = column(readers * RCAP + rank)
    table_row = column(((rows // 128) * 2 + rows % 2) * CX + (rows // 2) % CX)
    slots = iota((n, 256), 1)
    return jnp.sum(jnp.where(slot == slots, table_row - ROWS, 0), axis=0, keepdims=True) + ROWS


def fibre_ranks(code):
    masks = [code == c for c in range(9)]
    ones = jnp.concatenate([m.astype(F32) for m in masks], axis=0).astype(BF16)
    tri = (iota((128, 128), 0) < iota((128, 128), 1)).astype(BF16)
    before = jnp.dot(ones, tri, preferred_element_type=F32)
    total = jnp.dot(ones, jnp.ones((128, 128), BF16), preferred_element_type=F32)
    low = (iota((32, 32), 1) < iota((32, 32), 0)).astype(BF16)
    rank = jnp.zeros((32, 128), F32)
    for c in range(9):
        part = total[32 * c : 32 * c + 32]
        above = jnp.dot(low, part.astype(BF16), preferred_element_type=F32)
        rank = jnp.where(masks[c], before[32 * c : 32 * c + 32] + above, rank)
        if c == 4:
            stay = jnp.sum(part, axis=0, keepdims=True)[:, 0:1]
    return rank.astype(I32), stay.astype(I32)


def as_row(x):
    return jnp.concatenate([x[r : r + 1] for r in range(x.shape[0])], axis=1)


def compact(records, shift, stay):
    shape = records.shape
    n = shape[1]
    for b in range(11):
        w = 1 << b
        came_shift = pltpu.roll(shift, n - w, 1)
        came = pltpu.roll(records, n - w, 1)
        arrive = (came_shift & w) != 0
        leave = (shift & w) != 0
        records = jnp.where(arrive, came, records)
        shift = jnp.where(arrive, came_shift, jnp.where(leave, 0, shift))
    return jnp.where(iota(shape, 1) < stay, records, 0.0)


def pack_fibres(fibres_ref, code_ref, split_ref, pieces_ref, arrived_ref):
    code = code_ref[...]
    rank, stay = fibre_ranks(code)
    fibre = iota((32, 128), 0) * 128 + iota((32, 128), 1)
    shift = as_row(jnp.where(code == 4, fibre - rank, 0))
    slot = as_row(jnp.where(code == 4, -1, jnp.where(code < 4, code, code - 1) * CAP + rank))
    split_ref[...] = jnp.zeros(split_ref.shape, F32)
    for i, part in enumerate(split3(fibres_ref[...])):
        split_ref[8 * i : 8 * i + 6, :] = part
    acc = jnp.zeros((24, 8 * CAP), F32)
    step = 512
    for k in range(FIB_DEV // step):
        onehot = (iota((8 * CAP, step), 0) == slot[:, k * step : k * step + step]).astype(F32).astype(BF16)
        acc = acc + lax.dot_general(
            split_ref[:, k * step : k * step + step].astype(BF16),
            onehot,
            (((1,), (1,)), ((), ())),
            preferred_element_type=F32,
        )
    packed = acc[0:6] + acc[8:14] + acc[16:22]
    for j in range(8):
        pieces_ref[j] = packed[:, j * CAP : j * CAP + CAP]
    records = fibres_ref[...]
    arrived_ref[:, 4 * CAP : 4 * CAP + FIB_DEV] = compact(records, jnp.broadcast_to(shift, records.shape), stay)


def halo_kernel(
    sizes, velocity, fibres, code, rows, readers,
    zlo, zhi, xlo, xhi, corner, arrived, slots,
    split, pieces, halo_send, halo_recv, fib_send, fib_recv,
):
    nx, nz = sizes
    ix, iz = lax.axis_index("gx"), lax.axis_index("gz")

    def at(dx, dz):
        return (lax.rem(ix + dx + nx, nx), lax.rem(iz + dz + nz, nz))

    around = [(dx, dz) for dx in (-1, 0, 1) for dz in (-1, 0, 1) if (dx, dz) != (0, 0)]
    barrier = pltpu.get_barrier_semaphore()
    for dx, dz in around:
        pl.semaphore_signal(barrier, inc=1, device_id=at(dx, dz), device_id_type=MESH)
    pl.semaphore_wait(barrier, 8)

    copies = []

    def send(src, dst, dx, dz):
        i = len(copies)
        copy = pltpu.make_async_remote_copy(
            src, dst, halo_send.at[i], halo_recv.at[i], device_id=at(dx, dz), device_id_type=MESH
        )
        copy.start()
        copies.append(copy)

    send(velocity.at[:, 13:16], zlo, 0, 1)
    send(velocity.at[:, 0:3], zhi, 0, -1)
    send(velocity.at[:, :, 56:64], xlo, 1, 0)
    send(velocity.at[:, :, 0:8], xhi, -1, 0)
    send(velocity.at[:, 14:16, 56:64], corner.at[0], 1, 1)
    send(velocity.at[:, 14:16, 0:8], corner.at[1], -1, 1)
    send(velocity.at[:, 0:2, 56:64], corner.at[2], 1, -1)
    send(velocity.at[:, 0:2, 0:8], corner.at[3], -1, -1)

    pack_fibres(fibres, code, split, pieces, arrived)
    moved = []
    for j, (dx, dz) in enumerate(around):
        off = code_offset((dx + 1) * 3 + dz + 1)
        copy = pltpu.make_async_remote_copy(
            pieces.at[j], arrived.at[:, off : off + CAP], fib_send.at[j], fib_recv.at[j],
            device_id=at(dx, dz), device_id_type=MESH,
        )
        copy.start()
        moved.append(copy)
    slots[...] = slot_list(rows, readers)
    for copy in copies + moved:
        copy.wait()


def any_spec():
    return pl.BlockSpec(memory_space=pl.ANY)


def vmem_spec():
    return pl.BlockSpec(memory_space=pltpu.VMEM)


def halo_call(sizes, velocity, fibres, code, rows, readers):
    return pl.pallas_call(
        functools.partial(halo_kernel, sizes),
        out_shape=(
            jax.ShapeDtypeStruct((3, 3, CX, NY), F32),
            jax.ShapeDtypeStruct((3, 3, CX, NY), F32),
            jax.ShapeDtypeStruct((3, CZ, 8, NY), F32),
            jax.ShapeDtypeStruct((3, CZ, 8, NY), F32),
            jax.ShapeDtypeStruct((4, 3, 2, 8, NY), F32),
            jax.ShapeDtypeStruct((6, SLOT_DEV), F32),
            jax.ShapeDtypeStruct((1, 256), I32),
        ),
        in_specs=[any_spec()] + [vmem_spec()] * 4,
        out_specs=(any_spec(),) * 5 + (vmem_spec(),) * 2,
        scratch_shapes=[
            pltpu.VMEM((24, FIB_DEV), F32),
            pltpu.VMEM((8, 6, CAP), F32),
            pltpu.SemaphoreType.DMA((8,)),
            pltpu.SemaphoreType.DMA((8,)),
            pltpu.SemaphoreType.DMA((8,)),
            pltpu.SemaphoreType.DMA((8,)),
        ],
        compiler_params=pltpu.CompilerParams(
            collective_id=0, has_side_effects=True, vmem_limit_bytes=40 * MIB
        ),
        name="halo_and_fibres",
    )(velocity, fibres, code, rows, readers)


def beside(plane):
    lane = iota(plane.shape, 1)
    xp = pltpu.roll(plane, XW - 1, 0)
    xm = pltpu.roll(plane, 1, 0)
    yp = jnp.where(lane == NY - 1, 0.0, pltpu.roll(plane, NY - 1, 1))
    ym = jnp.where(lane == 0, 0.0, pltpu.roll(plane, 1, 1))
    return xp, xm, yp, ym


def transport_kernel(slots, velocity, zlo, zhi, xlo, xhi, corner, flow, out, send, first, second, third, grads):
    first[3:19, 0:64, :] = velocity[0]
    first[0:3, 0:64, :] = zlo[0]
    first[19:22, 0:64, :] = zhi[0]
    sub = iota((1, 8, NY), 1) < 4
    first[3:19, 64:72, :] = jnp.where(sub, xhi[0], xlo[0])
    first[1:3, 64:72, :] = jnp.where(sub, corner[1, 0], corner[0, 0])
    first[19:21, 64:72, :] = jnp.where(sub, corner[3, 0], corner[2, 0])

    ahead = DIFFUSION - 0.5 * ADVECTION * flow[...]
    behind = DIFFUSION + 0.5 * ADVECTION * flow[...]

    def advance(old, new, count):
        @pl.loop(0, count)
        def _(z):
            centre = old[z + 1]
            xp, xm, yp, ym = beside(centre)
            near = old[z] + old[z + 2] + yp + ym
            new[z] = (1.0 - 6.0 * DIFFUSION) * centre + DIFFUSION * near + ahead * xp + behind * xm

    advance(first, second, 20)
    advance(second, third, 18)
    grads[:, ROWS : ROWS + 8, :] = jnp.zeros((3, 8, 128), F32)

    @pl.loop(0, CZ)
    def _(z):
        centre = third[z + 1]
        out[0, z] = centre[0:64]
        xp, xm, yp, ym = beside(centre)
        along_z = third[z + 2] - third[z]
        for j, d in enumerate((xp - xm, yp - ym, along_z)):
            d = 0.5 * d
            for h in range(2):
                base = pl.multiple_of((z * 2 + h) * CX, CX)
                grads[j, pl.ds(base, CX), :] = d[0:64, h * 128 : h * 128 + 128]

    @pl.loop(0, 32)
    def _(g):
        base = pl.multiple_of(g * 8, 8)
        for k in range(8):
            row = slots[0, base + k]
            for j in range(3):
                send[j, pl.ds(base + k, 1), :] = grads[j, pl.ds(row, 1), :]


def transport_call(slots, velocity, zlo, zhi, xlo, xhi, corner, flow):
    return pl.pallas_call(
        transport_kernel,
        grid=(3,),
        out_shape=(
            jax.ShapeDtypeStruct((3, CZ, CX, NY), F32),
            jax.ShapeDtypeStruct((9, 256, 128), F32),
        ),
        in_specs=[
            pl.BlockSpec(memory_space=pltpu.SMEM),
            pl.BlockSpec((1, CZ, CX, NY), lambda c: (c, 0, 0, 0)),
            pl.BlockSpec((1, 3, CX, NY), lambda c: (c, 0, 0, 0)),
            pl.BlockSpec((1, 3, CX, NY), lambda c: (c, 0, 0, 0)),
            pl.BlockSpec((1, CZ, 8, NY), lambda c: (c, 0, 0, 0)),
            pl.BlockSpec((1, CZ, 8, NY), lambda c: (c, 0, 0, 0)),
            pl.BlockSpec((4, 1, 2, 8, NY), lambda c: (0, c, 0, 0, 0)),
            pl.BlockSpec((1, NY), lambda c: (0, 0)),
        ],
        out_specs=(
            pl.BlockSpec((1, CZ, CX, NY), lambda c: (c, 0, 0, 0)),
            pl.BlockSpec((3, 256, 128), lambda c: (c, 0, 0)),
        ),
        scratch_shapes=[
            pltpu.VMEM((22, XW, NY), F32),
            pltpu.VMEM((20, XW, NY), F32),
            pltpu.VMEM((18, XW, NY), F32),
            pltpu.VMEM((3, ROWS + 8, 128), F32),
        ],
        compiler_params=pltpu.CompilerParams(vmem_limit_bytes=40 * MIB),
        name="transport_and_rows",
    )(slots, velocity, zlo, zhi, xlo, xhi, corner, flow)


def exchange_kernel(sizes, send, recv, send_sem, recv_sem, own_sem):
    nx, nz = sizes
    count = nx * nz
    me = lax.axis_index("gx") * nz + lax.axis_index("gz")
    barrier = pltpu.get_barrier_semaphore()

    @pl.loop(1, count)
    def _(i):
        there = place(lax.rem(me + i, count), nz)
        pl.semaphore_signal(barrier, inc=1, device_id=there, device_id_type=MESH)

    pl.semaphore_wait(barrier, count - 1)
    own = pltpu.make_async_copy(send.at[:, me], recv.at[:, me], own_sem)
    own.start()

    @pl.loop(1, count)
    def _(i):
        reader = lax.rem(me + i, count)
        pltpu.make_async_remote_copy(
            send.at[:, reader], recv.at[:, me], send_sem, recv_sem,
            device_id=place(reader, nz), device_id_type=MESH,
        ).start()

    others = pl.ds(0, count - 1)
    pltpu.make_async_copy(recv.at[:, others], recv.at[:, others], recv_sem).wait()
    pltpu.make_async_copy(send.at[:, others], send.at[:, others], send_sem).wait()
    own.wait()


def exchange_call(sizes, send):
    return pl.pallas_call(
        functools.partial(exchange_kernel, sizes),
        out_shape=jax.ShapeDtypeStruct(send.shape, F32),
        in_specs=[any_spec()],
        out_specs=any_spec(),
        scratch_shapes=[pltpu.SemaphoreType.DMA] * 3,
        compiler_params=pltpu.CompilerParams(collective_id=1, has_side_effects=True),
        name="row_exchange",
    )(send)


def jeffery(orient, tensor):
    along = [sum(tensor[3 * i + j] * orient[j] for j in range(3)) for i in range(3)]
    across = [sum(tensor[3 * j + i] * orient[j] for j in range(3)) for i in range(3)]
    stretch = sum(orient[i] * along[i] for i in range(3))
    turned = []
    for i in range(3):
        strain = 0.5 * (along[i] + across[i])
        rotation = 0.5 * (along[i] - across[i])
        turned.append(orient[i] + TURN_STEP * (rotation + SHAPE_FACTOR * (strain - stretch * orient[i])))
    return turned


def turn_kernel(recv, cell, arrived, out, table):
    for q in range(9):
        block = jnp.transpose(recv[q])
        hi = block.astype(BF16)
        table[128 * q : 128 * q + 128, 0:256] = hi
        table[128 * q : 128 * q + 128, 256:512] = (block - hi.astype(F32)).astype(BF16)
    width = 256

    @pl.loop(0, SLOT_DEV // width)
    def _(k):
        base = pl.multiple_of(k * width, width)
        here = cell[:, pl.ds(base, width)]
        onehot = (iota((256, width), 0) == here // 128).astype(F32).astype(BF16)
        picked = jnp.dot(table[...], jnp.concatenate([onehot, onehot], axis=0), preferred_element_type=F32)
        lane = iota((128, width), 0) == here % 128
        tensor = [
            jnp.sum(jnp.where(lane, picked[128 * q : 128 * q + 128], 0.0), axis=0, keepdims=True) for q in range(9)
        ]
        records = arrived[:, pl.ds(base, width)]
        turned = jeffery([records[3 + i : 4 + i] for i in range(3)], tensor)
        out[0:3, pl.ds(base, width)] = records[0:3]
        for i in range(3):
            out[3 + i : 4 + i, pl.ds(base, width)] = turned[i]


def turn_call(recv, cell, arrived):
    return pl.pallas_call(
        turn_kernel,
        out_shape=jax.ShapeDtypeStruct((6, SLOT_DEV), F32),
        in_specs=[vmem_spec()] * 3,
        out_specs=vmem_spec(),
        scratch_shapes=[pltpu.VMEM((1152, 512), BF16)],
        compiler_params=pltpu.CompilerParams(vmem_limit_bytes=40 * MIB),
        name="gather_and_turn",
    )(recv, cell, arrived)


def per_device(sizes, velocity, mean_flow, fibres, moves, grad_rows, grad_readers, fibre_cell):
    count = sizes[0] * sizes[1]
    zlo, zhi, xlo, xhi, corner, arrived, slots = halo_call(
        sizes, velocity, fibres, moves.reshape(32, 128), grad_rows.reshape(1, -1), grad_readers.reshape(1, -1)
    )
    flow, send = transport_call(slots, velocity, zlo, zhi, xlo, xhi, corner, mean_flow.reshape(1, NY))
    recv = exchange_call(sizes, send.reshape(9, count, RCAP, 128))
    out = turn_call(recv.reshape(9, count * RCAP, 128), fibre_cell.reshape(1, SLOT_DEV), arrived)
    return flow, out


def solution(mesh):
    return jax.shard_map(
        functools.partial(per_device, (mesh.shape["gx"], mesh.shape["gz"])),
        mesh=mesh,
        in_specs=(
            P(None, "gz", "gx", None),
            P(),
            P(None, ("gx", "gz")),
            P(("gx", "gz"), None),
            P(("gx", "gz")),
            P(("gx", "gz"), None),
            P(("gx", "gz")),
        ),
        out_specs=(P(None, "gz", "gx", None), P(None, ("gx", "gz"))),
        check_vma=False,
    )
```

```python
import functools

import jax
import jax.numpy as jnp
from jax import lax
from jax.experimental import pallas as pl
from jax.experimental.pallas import tpu as pltpu
from jax.sharding import PartitionSpec as P

FIB_DEV = 4096
CAP = 128
SLOT_DEV = 5120
RCAP = 2
CX, CZ, NY = 64, 16, 256
XW = 72
ROWS = 2048

DIFFUSION = 0.1
ADVECTION = 0.4
SHAPE_FACTOR = 0.9
TURN_STEP = 0.25

MESH = pl.DeviceIdType.MESH
F32 = jnp.float32
BF16 = jnp.bfloat16
I32 = jnp.int32
MIB = 2**20


def code_offset(code):
    return code * CAP if code <= 4 else FIB_DEV + (code - 1) * CAP


def place(device, gz_size):
    return (device // gz_size, lax.rem(device, gz_size))


def split3(x):
    hi = x.astype(BF16).astype(F32)
    mid = (x - hi).astype(BF16).astype(F32)
    return hi, mid, x - hi - mid


def iota(shape, dim):
    return lax.broadcasted_iota(I32, shape, dim)


def slot_list(rows_ref, readers_ref):
    n = rows_ref.shape[1]
    rows, readers = rows_ref[...], readers_ref[...]
    sub, lane = iota((n, n), 0), iota((n, n), 1)
    diag = sub == lane

    def column(row):
        return jnp.sum(jnp.where(diag, jnp.broadcast_to(row, (n, n)), 0), axis=1, keepdims=True)

    same = (column(readers) == readers) & (sub < lane)
    rank = jnp.sum(same.astype(I32), axis=0, keepdims=True)
    slot = column(readers * RCAP + rank)
    table_row = column(((rows // 128) * 2 + rows % 2) * CX + (rows // 2) % CX)
    slots = iota((n, 256), 1)
    return jnp.sum(jnp.where(slot == slots, table_row - ROWS, 0), axis=0, keepdims=True) + ROWS


def fibre_ranks(code):
    masks = [code == c for c in range(9)]
    ones = jnp.concatenate([m.astype(F32) for m in masks], axis=0).astype(BF16)
    tri = (iota((128, 128), 0) < iota((128, 128), 1)).astype(BF16)
    before = jnp.dot(ones, tri, preferred_element_type=F32)
    total = jnp.dot(ones, jnp.ones((128, 128), BF16), preferred_element_type=F32)
    low = (iota((32, 32), 1) < iota((32, 32), 0)).astype(BF16)
    rank = jnp.zeros((32, 128), F32)
    for c in range(9):
        part = total[32 * c : 32 * c + 32]
        above = jnp.dot(low, part.astype(BF16), preferred_element_type=F32)
        rank = jnp.where(masks[c], before[32 * c : 32 * c + 32] + above, rank)
        if c == 4:
            stay = jnp.sum(part, axis=0, keepdims=True)[:, 0:1]
    return rank.astype(I32), stay.astype(I32)


def as_row(x):
    return jnp.concatenate([x[r : r + 1] for r in range(x.shape[0])], axis=1)


def compact(records, shift, stay):
    shape = records.shape
    n = shape[1]
    for b in range(11):
        w = 1 << b
        came_shift = pltpu.roll(shift, n - w, 1)
        came = pltpu.roll(records, n - w, 1)
        arrive = (came_shift & w) != 0
        leave = (shift & w) != 0
        records = jnp.where(arrive, came, records)
        shift = jnp.where(arrive, came_shift, jnp.where(leave, 0, shift))
    return jnp.where(iota(shape, 1) < stay, records, 0.0)


def pack_fibres(fibres_ref, code_ref, split_ref, pieces_ref, arrived_ref):
    code = code_ref[...]
    rank, stay = fibre_ranks(code)
    fibre = iota((32, 128), 0) * 128 + iota((32, 128), 1)
    shift = as_row(jnp.where(code == 4, fibre - rank, 0))
    slot = as_row(jnp.where(code == 4, -1, jnp.where(code < 4, code, code - 1) * CAP + rank))
    split_ref[...] = jnp.zeros(split_ref.shape, F32)
    for i, part in enumerate(split3(fibres_ref[...])):
        split_ref[8 * i : 8 * i + 6, :] = part
    acc = jnp.zeros((24, 8 * CAP), F32)
    step = 512
    for k in range(FIB_DEV // step):
        onehot = (iota((8 * CAP, step), 0) == slot[:, k * step : k * step + step]).astype(F32).astype(BF16)
        acc = acc + lax.dot_general(
            split_ref[:, k * step : k * step + step].astype(BF16),
            onehot,
            (((1,), (1,)), ((), ())),
            preferred_element_type=F32,
        )
    packed = acc[0:6] + acc[8:14] + acc[16:22]
    for j in range(8):
        pieces_ref[j] = packed[:, j * CAP : j * CAP + CAP]
    records = fibres_ref[...]
    arrived_ref[:, 4 * CAP : 4 * CAP + FIB_DEV] = compact(records, jnp.broadcast_to(shift, records.shape), stay)


def advance(old, new, count, ahead, behind, unroll):
    @pl.loop(0, count, unroll=unroll)
    def _(z):
        centre = old[z + 1]
        xp, xm, yp, ym = beside(centre)
        near = (old[z] + old[z + 2]) + (yp + ym)
        new[z] = (1.0 - 6.0 * DIFFUSION) * centre + DIFFUSION * near + (ahead * xp + behind * xm)


def beside(plane):
    lane = iota(plane.shape, 1)
    xp = pltpu.roll(plane, XW - 1, 0)
    xm = pltpu.roll(plane, 1, 0)
    yp = jnp.where(lane == NY - 1, 0.0, pltpu.roll(plane, NY - 1, 1))
    ym = jnp.where(lane == 0, 0.0, pltpu.roll(plane, 1, 1))
    return xp, xm, yp, ym


def flow_kernel(
    sizes, velocity, flow_hbm, fibres_hbm, code_hbm, rows_hbm, readers_hbm,
    out, recv_out, arrived_out,
    first, second, third, grads, send, recv, side, corner,
    flow, fibres, code, rows, readers, split, pieces, arrived, slots, slots_smem,
    load_sem, small_sem, slot_sem, out_sem, halo_send, halo_recv, fib_send, fib_recv,
    row_send, row_recv, row_own, last_sem,
):
    nx, nz = sizes
    count = nx * nz
    ix, iz = lax.axis_index("gx"), lax.axis_index("gz")
    me = ix * nz + iz

    def at(dx, dz):
        return (lax.rem(ix + dx + nx, nx), lax.rem(iz + dz + nz, nz))

    barrier = pltpu.get_barrier_semaphore()

    @pl.loop(1, count)
    def _(i):
        there = place(lax.rem(me + i, count), nz)
        pl.semaphore_signal(barrier, inc=1, device_id=there, device_id_type=MESH)

    small = [
        pltpu.make_async_copy(src, dst, small_sem.at[i])
        for i, (src, dst) in enumerate(
            ((rows_hbm, rows), (readers_hbm, readers), (code_hbm, code), (fibres_hbm, fibres), (flow_hbm, flow))
        )
    ]
    for copy in small:
        copy.start()
    loads = [
        pltpu.make_async_copy(velocity.at[c], first.at[c, 3:19, 0:64], load_sem.at[c]) for c in range(3)
    ]
    for copy in loads:
        copy.start()
    pl.semaphore_wait(barrier, count - 1)

    halos = []
    for c in range(3):
        part = []
        for i, (src, dst, dx, dz) in enumerate((
            (velocity.at[c, 13:16], first.at[c, 0:3, 0:64], 0, 1),
            (velocity.at[c, 0:3], first.at[c, 19:22, 0:64], 0, -1),
            (velocity.at[c, :, 56:64], side.at[c, 0], 1, 0),
            (velocity.at[c, :, 0:8], side.at[c, 1], -1, 0),
            (velocity.at[c, 14:16, 56:64], corner.at[c, 0], 1, 1),
            (velocity.at[c, 14:16, 0:8], corner.at[c, 1], -1, 1),
            (velocity.at[c, 0:2, 56:64], corner.at[c, 2], 1, -1),
            (velocity.at[c, 0:2, 0:8], corner.at[c, 3], -1, -1),
        )):
            copy = pltpu.make_async_remote_copy(
                src, dst, halo_send.at[8 * c + i], halo_recv.at[8 * c + i], device_id=at(dx, dz), device_id_type=MESH
            )
            copy.start()
            part.append(copy)
        halos.append(part)

    small[0].wait()
    small[1].wait()
    slots[...] = slot_list(rows, readers)
    to_scalars = pltpu.make_async_copy(slots, slots_smem, slot_sem)
    to_scalars.start()
    small[2].wait()
    small[3].wait()
    pack_fibres(fibres, code, split, pieces, arrived)
    moved = []
    around = [(dx, dz) for dx in (-1, 0, 1) for dz in (-1, 0, 1) if (dx, dz) != (0, 0)]
    for j, (dx, dz) in enumerate(around):
        off = code_offset((dx + 1) * 3 + dz + 1)
        copy = pltpu.make_async_remote_copy(
            pieces.at[j], arrived.at[:, off : off + CAP], fib_send.at[j], fib_recv.at[j],
            device_id=at(dx, dz), device_id_type=MESH,
        )
        copy.start()
        moved.append(copy)
    small[4].wait()
    to_scalars.wait()

    ahead = DIFFUSION - 0.5 * ADVECTION * flow[...]
    behind = DIFFUSION + 0.5 * ADVECTION * flow[...]
    sub = iota((1, 8, NY), 1) < 4
    grads[:, ROWS : ROWS + 8, :] = jnp.zeros((3, 8, 128), F32)
    outs, owns = [], []
    for c in range(3):
        loads[c].wait()
        for copy in halos[c]:
            copy.wait_recv()
        here, done = first.at[c], third.at[c]
        here[3:19, 64:72, :] = jnp.where(sub, side[c, 1], side[c, 0])
        here[1:3, 64:72, :] = jnp.where(sub, corner[c, 1], corner[c, 0])
        here[19:21, 64:72, :] = jnp.where(sub, corner[c, 3], corner[c, 2])
        advance(here, second, 20, ahead, behind, 5)
        advance(second, done, 18, ahead, behind, 6)
        copy = pltpu.make_async_copy(done.at[1:17, 0:64], out.at[c], out_sem.at[c])
        copy.start()
        outs.append(copy)

        @pl.loop(0, CZ, unroll=4)
        def _(z):
            xp, xm, yp, ym = beside(done[z + 1])
            along_z = done[z + 2] - done[z]
            for j, d in enumerate((xp - xm, yp - ym, along_z)):
                d = 0.5 * d
                for h in range(2):
                    base = pl.multiple_of((z * 2 + h) * CX, CX)
                    grads[j, pl.ds(base, CX), :] = d[0:64, h * 128 : h * 128 + 128]

        @pl.loop(0, count, unroll=4)
        def _(t):
            for k in range(RCAP):
                row = slots_smem[0, RCAP * t + k]
                for j in range(3):
                    send[c, t, 3 * k + j : 3 * k + j + 1, :] = grads[j, pl.ds(row, 1), :]

        own = pltpu.make_async_copy(send.at[c, me, 0:6], recv.at[c, me, 0:6], row_own.at[c])
        own.start()
        owns.append(own)

        @pl.loop(1, count)
        def _(i):
            reader = lax.rem(me + i, count)
            pltpu.make_async_remote_copy(
                send.at[c, reader, 0:6], recv.at[c, me, 0:6], row_send.at[c], row_recv.at[c],
                device_id=place(reader, nz), device_id_type=MESH,
            ).start()

    for copy in moved:
        copy.wait()
    last = [pltpu.make_async_copy(arrived, arrived_out, last_sem.at[3])]
    last[0].start()
    for c in range(3):
        every = pl.ds(0, count - 1)
        pltpu.make_async_copy(recv.at[c, every, 0:6], recv.at[c, every, 0:6], row_recv.at[c]).wait()
        owns[c].wait()
        copy = pltpu.make_async_copy(recv.at[c], recv_out.at[c], last_sem.at[c])
        copy.start()
        last.append(copy)
    for c in range(3):
        every = pl.ds(0, count - 1)
        pltpu.make_async_copy(send.at[c, every, 0:6], send.at[c, every, 0:6], row_send.at[c]).wait()
        outs[c].wait()
        for copy in halos[c]:
            copy.wait_send()
    for copy in last:
        copy.wait()


def hbm_spec():
    return pl.BlockSpec(memory_space=pltpu.HBM)


def any_spec():
    return pl.BlockSpec(memory_space=pl.ANY)


def vmem_spec():
    return pl.BlockSpec(memory_space=pltpu.VMEM)


def flow_call(sizes, *operands):
    count = sizes[0] * sizes[1]
    dma = pltpu.SemaphoreType.DMA
    return pl.pallas_call(
        functools.partial(flow_kernel, sizes),
        out_shape=(
            jax.ShapeDtypeStruct((3, CZ, CX, NY), F32),
            jax.ShapeDtypeStruct((3, count, 8, 128), F32),
            jax.ShapeDtypeStruct((6, SLOT_DEV), F32),
        ),
        in_specs=[hbm_spec()] * 6,
        out_specs=(hbm_spec(),) * 3,
        scratch_shapes=[
            pltpu.VMEM((3, 22, XW, NY), F32),
            pltpu.VMEM((20, XW, NY), F32),
            pltpu.VMEM((3, 18, XW, NY), F32),
            pltpu.VMEM((3, ROWS + 8, 128), F32),
            pltpu.VMEM((3, count, 8, 128), F32),
            pltpu.VMEM((3, count, 8, 128), F32),
            pltpu.VMEM((3, 2, CZ, 8, NY), F32),
            pltpu.VMEM((3, 4, 2, 8, NY), F32),
            pltpu.VMEM((1, NY), F32),
            pltpu.VMEM((6, FIB_DEV), F32),
            pltpu.VMEM((32, 128), I32),
            pltpu.VMEM((1, 192), I32),
            pltpu.VMEM((1, 192), I32),
            pltpu.VMEM((24, FIB_DEV), F32),
            pltpu.VMEM((8, 6, CAP), F32),
            pltpu.VMEM((6, SLOT_DEV), F32),
            pltpu.VMEM((1, 256), I32),
            pltpu.SMEM((1, 256), I32),
            dma((3,)), dma((5,)), dma, dma((3,)), dma((24,)), dma((24,)), dma((8,)), dma((8,)),
            dma((3,)), dma((3,)), dma((3,)), dma((4,)),
        ],
        compiler_params=pltpu.CompilerParams(
            collective_id=0, has_side_effects=True, vmem_limit_bytes=60 * MIB
        ),
        name="flow_and_rows",
    )(*operands)


def jeffery(orient, tensor):
    along = [sum(tensor[3 * i + j] * orient[j] for j in range(3)) for i in range(3)]
    across = [sum(tensor[3 * j + i] * orient[j] for j in range(3)) for i in range(3)]
    stretch = sum(orient[i] * along[i] for i in range(3))
    turned = []
    for i in range(3):
        strain = 0.5 * (along[i] + across[i])
        rotation = 0.5 * (along[i] - across[i])
        turned.append(orient[i] + TURN_STEP * (rotation + SHAPE_FACTOR * (strain - stretch * orient[i])))
    return turned


def turn_kernel(recv, cell, arrived, flow, out, flow_out, table, flow_sem):
    copy = pltpu.make_async_copy(flow, flow_out, flow_sem)
    copy.start()
    count = recv.shape[1]
    for c in range(3):
        rows = recv.at[c].reshape(count * 8, 128)
        for j in range(3):
            q = 3 * c + j
            for k in range(RCAP):
                block = jnp.transpose(rows[pl.ds(3 * k + j, count, 8), :])
                hi = block.astype(BF16)
                table[128 * q : 128 * q + 128, count * k : count * (k + 1)] = hi
                table[128 * q : 128 * q + 128, 256 + count * k : 256 + count * (k + 1)] = (
                    block - hi.astype(F32)
                ).astype(BF16)
    width = 256

    @pl.loop(0, SLOT_DEV // width)
    def _(n):
        base = pl.multiple_of(n * width, width)
        here = cell[:, pl.ds(base, width)]
        row = here // 128
        row = (row % RCAP) * count + row // RCAP
        onehot = (iota((256, width), 0) == row).astype(F32).astype(BF16)
        picked = jnp.dot(table[...], jnp.concatenate([onehot, onehot], axis=0), preferred_element_type=F32)
        lane = iota((128, width), 0) == here % 128
        tensor = [
            jnp.sum(jnp.where(lane, picked[128 * q : 128 * q + 128], 0.0), axis=0, keepdims=True) for q in range(9)
        ]
        records = arrived[:, pl.ds(base, width)]
        turned = jeffery([records[3 + i : 4 + i] for i in range(3)], tensor)
        out[0:3, pl.ds(base, width)] = records[0:3]
        for i in range(3):
            out[3 + i : 4 + i, pl.ds(base, width)] = turned[i]

    copy.wait()


def turn_call(recv, cell, arrived, flow):
    return pl.pallas_call(
        turn_kernel,
        out_shape=(jax.ShapeDtypeStruct((6, SLOT_DEV), F32), jax.ShapeDtypeStruct(flow.shape, F32)),
        in_specs=[vmem_spec()] * 3 + [any_spec()],
        out_specs=(vmem_spec(), hbm_spec()),
        scratch_shapes=[pltpu.VMEM((1152, 512), BF16), pltpu.SemaphoreType.DMA],
        compiler_params=pltpu.CompilerParams(vmem_limit_bytes=60 * MIB),
        name="gather_and_turn",
    )(recv, cell, arrived, flow)


def per_device(sizes, velocity, mean_flow, fibres, moves, grad_rows, grad_readers, fibre_cell):
    flow, recv, arrived = flow_call(
        sizes, velocity, mean_flow.reshape(1, NY), fibres, moves.reshape(32, 128),
        grad_rows.reshape(1, -1), grad_readers.reshape(1, -1),
    )
    out, flow = turn_call(recv, fibre_cell.reshape(1, SLOT_DEV), arrived, flow)
    return flow, out


def solution(mesh):
    return jax.shard_map(
        functools.partial(per_device, (mesh.shape["gx"], mesh.shape["gz"])),
        mesh=mesh,
        in_specs=(
            P(None, "gz", "gx", None),
            P(),
            P(None, ("gx", "gz")),
            P(("gx", "gz"), None),
            P(("gx", "gz")),
            P(("gx", "gz"), None),
            P(("gx", "gz")),
        ),
        out_specs=(P(None, "gz", "gx", None), P(None, ("gx", "gz"))),
        check_vma=False,
    )
```

```python
import functools

import jax
import jax.numpy as jnp
from jax import lax
from jax.experimental import pallas as pl
from jax.experimental.pallas import tpu as pltpu
from jax.sharding import PartitionSpec as P

FIB_DEV = 4096
CAP = 128
SLOT_DEV = 5120
RCAP = 2
CX, CZ, NY = 64, 16, 256
XW = 72
ROWS = 2048

DIFFUSION = 0.1
ADVECTION = 0.4
SHAPE_FACTOR = 0.9
TURN_STEP = 0.25

MESH = pl.DeviceIdType.MESH
F32 = jnp.float32
BF16 = jnp.bfloat16
I32 = jnp.int32
MIB = 2**20


def code_offset(code):
    return code * CAP if code <= 4 else FIB_DEV + (code - 1) * CAP


def place(device, gz_size):
    return (device // gz_size, lax.rem(device, gz_size))


def split3(x):
    hi = x.astype(BF16).astype(F32)
    mid = (x - hi).astype(BF16).astype(F32)
    return hi, mid, x - hi - mid


def iota(shape, dim):
    return lax.broadcasted_iota(I32, shape, dim)


def slot_list(rows_ref, readers_ref):
    n = rows_ref.shape[1]
    rows, readers = rows_ref[...], readers_ref[...]
    sub, lane = iota((n, n), 0), iota((n, n), 1)
    diag = sub == lane

    def column(row):
        return jnp.sum(jnp.where(diag, jnp.broadcast_to(row, (n, n)), 0), axis=1, keepdims=True)

    same = (column(readers) == readers) & (sub < lane)
    rank = jnp.sum(same.astype(I32), axis=0, keepdims=True)
    slot = column(readers * RCAP + rank)
    table_row = column(((rows // 128) * 2 + rows % 2) * CX + (rows // 2) % CX)
    slots = iota((n, 256), 1)
    return jnp.sum(jnp.where(slot == slots, table_row - ROWS, 0), axis=0, keepdims=True) + ROWS


def fibre_ranks(code):
    masks = [code == c for c in range(9)]
    ones = jnp.concatenate([m.astype(F32) for m in masks], axis=0).astype(BF16)
    tri = (iota((128, 128), 0) < iota((128, 128), 1)).astype(BF16)
    before = jnp.dot(ones, tri, preferred_element_type=F32)
    total = jnp.dot(ones, jnp.ones((128, 128), BF16), preferred_element_type=F32)
    low = (iota((32, 32), 1) < iota((32, 32), 0)).astype(BF16)
    rank = jnp.zeros((32, 128), F32)
    for c in range(9):
        part = total[32 * c : 32 * c + 32]
        above = jnp.dot(low, part.astype(BF16), preferred_element_type=F32)
        rank = jnp.where(masks[c], before[32 * c : 32 * c + 32] + above, rank)
        if c == 4:
            stay = jnp.sum(part, axis=0, keepdims=True)[:, 0:1]
    return rank.astype(I32), stay.astype(I32)


def as_row(x):
    return jnp.concatenate([x[r : r + 1] for r in range(x.shape[0])], axis=1)


def compact(records, shift, stay):
    shape = records.shape
    n = shape[1]
    for b in range(11):
        w = 1 << b
        came_shift = pltpu.roll(shift, n - w, 1)
        came = pltpu.roll(records, n - w, 1)
        arrive = (came_shift & w) != 0
        leave = (shift & w) != 0
        records = jnp.where(arrive, came, records)
        shift = jnp.where(arrive, came_shift, jnp.where(leave, 0, shift))
    return jnp.where(iota(shape, 1) < stay, records, 0.0)


def pack_fibres(fibres_ref, code_ref, split_ref, pieces_ref, arrived_ref):
    code = code_ref[...]
    rank, stay = fibre_ranks(code)
    fibre = iota((32, 128), 0) * 128 + iota((32, 128), 1)
    shift = as_row(jnp.where(code == 4, fibre - rank, 0))
    slot = as_row(jnp.where(code == 4, -1, jnp.where(code < 4, code, code - 1) * CAP + rank))
    split_ref[...] = jnp.zeros(split_ref.shape, F32)
    for i, part in enumerate(split3(fibres_ref[...])):
        split_ref[8 * i : 8 * i + 6, :] = part
    acc = jnp.zeros((24, 8 * CAP), F32)
    step = 512
    for k in range(FIB_DEV // step):
        onehot = (iota((8 * CAP, step), 0) == slot[:, k * step : k * step + step]).astype(F32).astype(BF16)
        acc = acc + lax.dot_general(
            split_ref[:, k * step : k * step + step].astype(BF16),
            onehot,
            (((1,), (1,)), ((), ())),
            preferred_element_type=F32,
        )
    packed = acc[0:6] + acc[8:14] + acc[16:22]
    for j in range(8):
        pieces_ref[j] = packed[:, j * CAP : j * CAP + CAP]
    records = fibres_ref[...]
    arrived_ref[:, 4 * CAP : 4 * CAP + FIB_DEV] = compact(records, jnp.broadcast_to(shift, records.shape), stay)


def advance(old, new, count, ahead, behind, unroll):
    @pl.loop(0, count, unroll=unroll)
    def _(z):
        centre = old[z + 1]
        xp, xm, yp, ym = beside(centre)
        near = (old[z] + old[z + 2]) + (yp + ym)
        new[z] = (1.0 - 6.0 * DIFFUSION) * centre + DIFFUSION * near + (ahead * xp + behind * xm)


def beside(plane):
    lane = iota(plane.shape, 1)
    xp = pltpu.roll(plane, XW - 1, 0)
    xm = pltpu.roll(plane, 1, 0)
    yp = jnp.where(lane == NY - 1, 0.0, pltpu.roll(plane, NY - 1, 1))
    ym = jnp.where(lane == 0, 0.0, pltpu.roll(plane, 1, 1))
    return xp, xm, yp, ym


def flow_kernel(
    sizes, velocity, flow_hbm, fibres_hbm, code_hbm, rows_hbm, readers_hbm, cell_hbm,
    out, recv_out, tensor_out, arrived_out,
    first, second, third, grads, send, recv, side, edge, corner,
    flow, fibres, code, rows, readers, cell, split, pieces, arrived, slots, slots_smem,
    onehot, table, tensor,
    load_sem, small_sem, slot_sem, out_sem, halo_send, halo_recv, fib_send, fib_recv,
    corner_send, corner_recv, row_send, row_recv, row_own, last_sem, known,
):
    nx, nz = sizes
    count = nx * nz
    ix, iz = lax.axis_index("gx"), lax.axis_index("gz")
    me = ix * nz + iz

    def at(dx, dz):
        return (lax.rem(ix + dx + nx, nx), lax.rem(iz + dz + nz, nz))

    around = [(dx, dz) for dx in (-1, 0, 1) for dz in (-1, 0, 1) if (dx, dz) != (0, 0)]

    def greet(semaphore, reach):
        there = {((dx * reach) % nx, (dz * reach) % nz) for dx, dz in around} - {(0, 0)}
        for dx, dz in sorted(there):
            pl.semaphore_signal(semaphore, inc=1, device_id=at(dx, dz), device_id_type=MESH)
        return len(there)

    barrier = pltpu.get_barrier_semaphore()
    greeted = greet(barrier, 1)

    loads = [
        pltpu.make_async_copy(velocity.at[c], first.at[c, 3:19, 0:64], load_sem.at[c]) for c in range(3)
    ]
    small = [
        pltpu.make_async_copy(src, dst, small_sem.at[i])
        for i, (src, dst) in enumerate((
            (rows_hbm, rows), (readers_hbm, readers), (code_hbm, code), (fibres_hbm, fibres), (flow_hbm, flow),
            (cell_hbm, cell),
        ))
    ]
    for copy in small + loads:
        copy.start()
    pl.semaphore_wait(barrier, greeted)

    def remote(src, dst, send_sem, recv_sem, dx, dz):
        copy = pltpu.make_async_remote_copy(
            src, dst, send_sem, recv_sem, device_id=at(dx, dz), device_id_type=MESH
        )
        copy.start()
        return copy

    def send_halo(c):
        faces = (
            (velocity.at[c, 13:16], first.at[c, 0:3, 0:64], 0, 1),
            (velocity.at[c, 0:3], first.at[c, 19:22, 0:64], 0, -1),
            (velocity.at[c, :, 56:64], side.at[c, 0], 1, 0),
            (velocity.at[c, :, 0:8], side.at[c, 1], -1, 0),
        )
        return [
            remote(src, dst, halo_send.at[4 * c + i], halo_recv.at[4 * c + i], dx, dz)
            for i, (src, dst, dx, dz) in enumerate(faces)
        ]

    halos = [send_halo(0)]
    small[0].wait()
    small[1].wait()
    slots[...] = slot_list(rows, readers)
    to_scalars = pltpu.make_async_copy(slots, slots_smem, slot_sem)
    to_scalars.start()
    greeted = greet(known.at[0], 1)

    for copy in loads:
        copy.wait()
    diagonal = [(1, 1), (-1, 1), (1, -1), (-1, -1)]
    corners = []
    for i, (dx, dz) in enumerate(diagonal):
        near, far = (18, 17) if dz == 1 else (3, 4)
        x1, x2 = (63, 62) if dx == 1 else (0, 1)
        for c in range(3):
            for r, (z, x) in enumerate(((near, x1), (near, x2), (far, x1))):
                edge[i, 3 * c + r] = first[c, z, x : x + 1, :]
        corners.append(remote(edge.at[i], corner.at[i], corner_send.at[i], corner_recv.at[i], dx, dz))

    pl.semaphore_wait(known.at[0], greeted)
    greeted = greet(known.at[1], 2)
    small[2].wait()
    small[3].wait()
    pack_fibres(fibres, code, split, pieces, arrived)
    moved = []
    for j, (dx, dz) in enumerate(around):
        off = code_offset((dx + 1) * 3 + dz + 1)
        moved.append(
            remote(pieces.at[j], arrived.at[:, off : off + CAP], fib_send.at[j], fib_recv.at[j], dx, dz)
        )
    halos.append(send_halo(1))
    pl.semaphore_wait(known.at[1], greeted)
    greeted = greet(known.at[2], 4)
    small[5].wait()
    width = 512

    @pl.loop(0, SLOT_DEV // width)
    def _(n):
        base = pl.multiple_of(n * width, width)
        onehot[:, pl.ds(base, width)] = row_onehot(cell[:, pl.ds(base, width)], count)

    small[4].wait()
    to_scalars.wait()
    ahead = DIFFUSION - 0.5 * ADVECTION * flow[...]
    behind = DIFFUSION + 0.5 * ADVECTION * flow[...]
    sub = iota((1, 8, NY), 1) < 4
    grads[:, ROWS : ROWS + 8, :] = jnp.zeros((3, 8, 128), F32)
    outs, owns = [], []
    for c in range(3):
        for copy in halos[c]:
            copy.wait_recv()
        if c == 0:
            halos.append(send_halo(2))
            for copy in corners:
                copy.wait_recv()
        here, done = first.at[c], third.at[c]
        here[3:19, 64:72, :] = jnp.where(sub, side[c, 1], side[c, 0])
        for i, (dx, dz) in enumerate(diagonal):
            near, far = (2, 1) if dz == 1 else (19, 20)
            x1, x2 = (71, 70) if dx == 1 else (64, 65)
            for r, (z, x) in enumerate(((near, x1), (near, x2), (far, x1))):
                here[z, x : x + 1, :] = corner[i, 3 * c + r]
        advance(here, second, 20, ahead, behind, 5)
        advance(second, done, 18, ahead, behind, 6)
        copy = pltpu.make_async_copy(done.at[1:17, 0:64], out.at[c], out_sem.at[c])
        copy.start()
        outs.append(copy)

        @pl.loop(0, CZ, unroll=4)
        def _(z):
            xp, xm, yp, ym = beside(done[z + 1])
            along_z = done[z + 2] - done[z]
            for j, d in enumerate((xp - xm, yp - ym, along_z)):
                d = 0.5 * d
                for h in range(2):
                    base = pl.multiple_of((z * 2 + h) * CX, CX)
                    grads[j, pl.ds(base, CX), :] = d[0:64, h * 128 : h * 128 + 128]

        @pl.loop(0, count, unroll=4)
        def _(t):
            for k in range(RCAP):
                row = slots_smem[0, RCAP * t + k]
                for j in range(3):
                    send[c, t, 3 * k + j : 3 * k + j + 1, :] = grads[j, pl.ds(row, 1), :]

        if c == 0:
            pl.semaphore_wait(known.at[2], greeted)
        own = pltpu.make_async_copy(send.at[c, me, 0:6], recv.at[c, me, 0:6], row_own.at[c])
        own.start()
        owns.append(own)

        @pl.loop(1, count)
        def _(i):
            reader = lax.rem(me + i, count)
            pltpu.make_async_remote_copy(
                send.at[c, reader, 0:6], recv.at[c, me, 0:6], row_send.at[c], row_recv.at[c],
                device_id=place(reader, nz), device_id_type=MESH,
            ).start()

    for copy in moved:
        copy.wait()
    last = [pltpu.make_async_copy(arrived, arrived_out, last_sem.at[0])]
    last[0].start()
    every = pl.ds(0, count - 1)
    for c in range(3):
        pltpu.make_async_copy(recv.at[c, every, 0:6], recv.at[c, every, 0:6], row_recv.at[c]).wait()
        owns[c].wait()
        if c < 2:
            fill_table(recv.at[c], table)
            width = 1024

            @pl.loop(0, SLOT_DEV // width)
            def _(n):
                part = pl.ds(pl.multiple_of(n * width, width), width)
                for j, row in enumerate(pick(table, onehot[:, part], cell[:, part])):
                    tensor[3 * c + j : 3 * c + j + 1, part] = row

    last.append(pltpu.make_async_copy(recv.at[2], recv_out, last_sem.at[1]))
    last.append(pltpu.make_async_copy(tensor, tensor_out, last_sem.at[2]))
    last[1].start()
    last[2].start()
    for c in range(3):
        pltpu.make_async_copy(send.at[c, every, 0:6], send.at[c, every, 0:6], row_send.at[c]).wait()
        outs[c].wait()
        for copy in halos[c]:
            copy.wait_send()
    for copy in corners:
        copy.wait_send()
    for copy in last:
        copy.wait()


def row_onehot(cell, count):
    row = cell // 128
    row = (row % RCAP) * count + row // RCAP
    return (iota((RCAP * count, cell.shape[1]), 0) == row).astype(F32).astype(BF16)


def fill_table(recv, table):
    count = recv.shape[0]
    flat = recv.reshape(count * 8, 128)
    for j in range(3):
        for k in range(RCAP):
            block = jnp.transpose(flat[pl.ds(3 * k + j, count, 8), :])
            hi = block.astype(BF16)
            at = count * k
            table[128 * j : 128 * j + 128, at : at + count] = hi
            at = at + RCAP * count
            table[128 * j : 128 * j + 128, at : at + count] = (block - hi.astype(F32)).astype(BF16)


def pick(table, onehot, cell):
    rows = jnp.dot(table[...], jnp.concatenate([onehot, onehot], axis=0), preferred_element_type=F32)
    lane = iota((128, cell.shape[1]), 0) == cell % 128
    return [jnp.sum(jnp.where(lane, rows[128 * j : 128 * j + 128], 0.0), axis=0, keepdims=True) for j in range(3)]


def hbm_spec():
    return pl.BlockSpec(memory_space=pltpu.HBM)


def any_spec():
    return pl.BlockSpec(memory_space=pl.ANY)


def vmem_spec():
    return pl.BlockSpec(memory_space=pltpu.VMEM)


def flow_call(sizes, *operands):
    count = sizes[0] * sizes[1]
    dma = pltpu.SemaphoreType.DMA
    return pl.pallas_call(
        functools.partial(flow_kernel, sizes),
        out_shape=(
            jax.ShapeDtypeStruct((3, CZ, CX, NY), F32),
            jax.ShapeDtypeStruct((count, 8, 128), F32),
            jax.ShapeDtypeStruct((6, SLOT_DEV), F32),
            jax.ShapeDtypeStruct((6, SLOT_DEV), F32),
        ),
        in_specs=[hbm_spec()] * 7,
        out_specs=(hbm_spec(),) * 4,
        scratch_shapes=[
            pltpu.VMEM((3, 22, XW, NY), F32),
            pltpu.VMEM((20, XW, NY), F32),
            pltpu.VMEM((3, 18, XW, NY), F32),
            pltpu.VMEM((3, ROWS + 8, 128), F32),
            pltpu.VMEM((3, count, 8, 128), F32),
            pltpu.VMEM((3, count, 8, 128), F32),
            pltpu.VMEM((3, 2, CZ, 8, NY), F32),
            pltpu.VMEM((4, 9, 1, NY), F32),
            pltpu.VMEM((4, 9, 1, NY), F32),
            pltpu.VMEM((1, NY), F32),
            pltpu.VMEM((6, FIB_DEV), F32),
            pltpu.VMEM((32, 128), I32),
            pltpu.VMEM((1, 192), I32),
            pltpu.VMEM((1, 192), I32),
            pltpu.VMEM((1, SLOT_DEV), I32),
            pltpu.VMEM((24, FIB_DEV), F32),
            pltpu.VMEM((8, 6, CAP), F32),
            pltpu.VMEM((6, SLOT_DEV), F32),
            pltpu.VMEM((1, 256), I32),
            pltpu.SMEM((1, 256), I32),
            pltpu.VMEM((RCAP * count, SLOT_DEV), BF16),
            pltpu.VMEM((384, 2 * RCAP * count), BF16),
            pltpu.VMEM((6, SLOT_DEV), F32),
            dma((3,)), dma((6,)), dma, dma((3,)), dma((12,)), dma((12,)), dma((8,)), dma((8,)),
            dma((4,)), dma((4,)), dma((3,)), dma((3,)), dma((3,)), dma((3,)), pltpu.SemaphoreType.REGULAR((3,)),
        ],
        compiler_params=pltpu.CompilerParams(
            collective_id=0, has_side_effects=True, vmem_limit_bytes=60 * MIB
        ),
        name="flow_and_rows",
    )(*operands)


def jeffery(orient, tensor):
    along = [sum(tensor[3 * i + j] * orient[j] for j in range(3)) for i in range(3)]
    across = [sum(tensor[3 * j + i] * orient[j] for j in range(3)) for i in range(3)]
    stretch = sum(orient[i] * along[i] for i in range(3))
    turned = []
    for i in range(3):
        strain = 0.5 * (along[i] + across[i])
        rotation = 0.5 * (along[i] - across[i])
        turned.append(orient[i] + TURN_STEP * (rotation + SHAPE_FACTOR * (strain - stretch * orient[i])))
    return turned


def turn_kernel(recv, tensor, cell, arrived, flow, out, flow_out, table, held, in_sem, out_sem):
    bring = pltpu.make_async_copy(flow, held, in_sem)
    bring.start()
    store = pltpu.make_async_copy(held, flow_out, out_sem)
    count = recv.shape[0]
    fill_table(recv, table)
    width = 1024

    def turn(n):
        part = pl.ds(pl.multiple_of(n * width, width), width)
        here = cell[:, part]
        rows = [tensor[i : i + 1, part] for i in range(6)] + pick(table, row_onehot(here, count), here)
        records = arrived[:, part]
        turned = jeffery([records[3 + i : 4 + i] for i in range(3)], rows)
        out[0:3, part] = records[0:3]
        for i in range(3):
            out[3 + i : 4 + i, part] = turned[i]

    turn(0)
    bring.wait()
    store.start()

    @pl.loop(1, SLOT_DEV // width)
    def _(n):
        turn(n)

    store.wait()


def turn_call(recv, tensor, cell, arrived, flow):
    return pl.pallas_call(
        turn_kernel,
        out_shape=(jax.ShapeDtypeStruct((6, SLOT_DEV), F32), jax.ShapeDtypeStruct(flow.shape, F32)),
        in_specs=[vmem_spec()] * 4 + [hbm_spec()],
        out_specs=(vmem_spec(), hbm_spec()),
        scratch_shapes=[
            pltpu.VMEM((384, 2 * RCAP * recv.shape[0]), BF16),
            pltpu.VMEM(flow.shape, F32),
            pltpu.SemaphoreType.DMA,
            pltpu.SemaphoreType.DMA,
        ],
        compiler_params=pltpu.CompilerParams(vmem_limit_bytes=60 * MIB),
        name="gather_and_turn",
    )(recv, tensor, cell, arrived, flow)


def per_device(sizes, velocity, mean_flow, fibres, moves, grad_rows, grad_readers, fibre_cell):
    cell = fibre_cell.reshape(1, SLOT_DEV)
    flow, recv, tensor, arrived = flow_call(
        sizes, velocity, mean_flow.reshape(1, NY), fibres, moves.reshape(32, 128),
        grad_rows.reshape(1, -1), grad_readers.reshape(1, -1), cell,
    )
    out, flow = turn_call(recv, tensor, cell, arrived, flow)
    return flow, out


def solution(mesh):
    return jax.shard_map(
        functools.partial(per_device, (mesh.shape["gx"], mesh.shape["gz"])),
        mesh=mesh,
        in_specs=(
            P(None, "gz", "gx", None),
            P(),
            P(None, ("gx", "gz")),
            P(("gx", "gz"), None),
            P(("gx", "gz")),
            P(("gx", "gz"), None),
            P(("gx", "gz")),
        ),
        out_specs=(P(None, "gz", "gx", None), P(None, ("gx", "gz"))),
        check_vma=False,
    )
```

```python
import functools

import jax
import jax.numpy as jnp
from jax import lax
from jax.experimental import pallas as pl
from jax.experimental.pallas import tpu as pltpu
from jax.sharding import PartitionSpec as P

FIB_DEV = 4096
CAP = 128
SLOT_DEV = 5120
RCAP = 2
CX, CZ, NY = 64, 16, 256
XW = 72
ROWS = 2048

DIFFUSION = 0.1
ADVECTION = 0.4
SHAPE_FACTOR = 0.9
TURN_STEP = 0.25

MESH = pl.DeviceIdType.MESH
F32 = jnp.float32
BF16 = jnp.bfloat16
I32 = jnp.int32
MIB = 2**20


def code_offset(code):
    return code * CAP if code <= 4 else FIB_DEV + (code - 1) * CAP


def place(device, gz_size):
    return (device // gz_size, lax.rem(device, gz_size))


def split3(x):
    hi = x.astype(BF16).astype(F32)
    mid = (x - hi).astype(BF16).astype(F32)
    return hi, mid, x - hi - mid


def iota(shape, dim):
    return lax.broadcasted_iota(I32, shape, dim)


def slot_list(rows_ref, readers_ref):
    n = rows_ref.shape[1]
    rows, readers = rows_ref[...], readers_ref[...]
    sub, lane = iota((n, n), 0), iota((n, n), 1)
    diag = sub == lane

    def column(row):
        return jnp.sum(jnp.where(diag, jnp.broadcast_to(row, (n, n)), 0), axis=1, keepdims=True)

    same = (column(readers) == readers) & (sub < lane)
    rank = jnp.sum(same.astype(I32), axis=0, keepdims=True)
    slot = column(readers * RCAP + rank)
    table_row = column(((rows // 128) * 2 + rows % 2) * CX + (rows // 2) % CX)
    slots = iota((n, 256), 1)
    return jnp.sum(jnp.where(slot == slots, table_row - ROWS, 0), axis=0, keepdims=True) + ROWS


def fibre_ranks(code):
    masks = [code == c for c in range(9)]
    ones = jnp.concatenate([m.astype(F32) for m in masks], axis=0).astype(BF16)
    tri = (iota((128, 128), 0) < iota((128, 128), 1)).astype(BF16)
    before = jnp.dot(ones, tri, preferred_element_type=F32)
    total = jnp.dot(ones, jnp.ones((128, 128), BF16), preferred_element_type=F32)
    low = (iota((32, 32), 1) < iota((32, 32), 0)).astype(BF16)
    rank = jnp.zeros((32, 128), F32)
    for c in range(9):
        part = total[32 * c : 32 * c + 32]
        above = jnp.dot(low, part.astype(BF16), preferred_element_type=F32)
        rank = jnp.where(masks[c], before[32 * c : 32 * c + 32] + above, rank)
        if c == 4:
            stay = jnp.sum(part, axis=0, keepdims=True)[:, 0:1]
    return rank.astype(I32), stay.astype(I32)


def as_row(x):
    return jnp.concatenate([x[r : r + 1] for r in range(x.shape[0])], axis=1)


def compact(records, shift, stay):
    shape = records.shape
    n = shape[1]
    for b in range(11):
        w = 1 << b
        came_shift = pltpu.roll(shift, n - w, 1)
        came = pltpu.roll(records, n - w, 1)
        arrive = (came_shift & w) != 0
        leave = (shift & w) != 0
        records = jnp.where(arrive, came, records)
        shift = jnp.where(arrive, came_shift, jnp.where(leave, 0, shift))
    return jnp.where(iota(shape, 1) < stay, records, 0.0)


def pack_fibres(fibres_ref, code_ref, split_ref, pieces_ref, arrived_ref):
    code = code_ref[...]
    rank, stay = fibre_ranks(code)
    fibre = iota((32, 128), 0) * 128 + iota((32, 128), 1)
    shift = as_row(jnp.where(code == 4, fibre - rank, 0))
    group = as_row(jnp.where(code == 4, -1, jnp.where(code < 4, code, code - 1)))
    rank = as_row(rank)
    split_ref[...] = jnp.zeros(split_ref.shape, F32)
    for i, part in enumerate(split3(fibres_ref[...])):
        split_ref[8 * i : 8 * i + 6, :] = part
    acc = jnp.zeros((8 * 24, CAP), F32)
    step = 1024
    for k in range(FIB_DEV // step):
        part = slice(k * step, k * step + step)
        values = split_ref[:, part]
        mine = jnp.concatenate([jnp.where(group[:, part] == j, values, 0.0) for j in range(8)], axis=0)
        onehot = (iota((CAP, step), 0) == rank[:, part]).astype(F32).astype(BF16)
        acc = acc + lax.dot_general(
            mine.astype(BF16), onehot, (((1,), (1,)), ((), ())), preferred_element_type=F32
        )
    for j in range(8):
        own = acc[24 * j : 24 * j + 24]
        pieces_ref[j] = own[0:6] + own[8:14] + own[16:22]
    records = fibres_ref[...]
    arrived_ref[:, 4 * CAP : 4 * CAP + FIB_DEV] = compact(records, jnp.broadcast_to(shift, records.shape), stay)


def advance(old, new, count, ahead, behind, unroll):
    @pl.loop(0, count, unroll=unroll)
    def _(z):
        centre = old[z + 1]
        xp, xm, yp, ym = beside(centre)
        near = (old[z] + old[z + 2]) + (yp + ym)
        new[z] = (1.0 - 6.0 * DIFFUSION) * centre + DIFFUSION * near + (ahead * xp + behind * xm)


def beside(plane):
    lane = iota(plane.shape, 1)
    xp = pltpu.roll(plane, XW - 1, 0)
    xm = pltpu.roll(plane, 1, 0)
    yp = jnp.where(lane == NY - 1, 0.0, pltpu.roll(plane, NY - 1, 1))
    ym = jnp.where(lane == 0, 0.0, pltpu.roll(plane, 1, 1))
    return xp, xm, yp, ym


def flow_kernel(
    sizes, velocity, flow_hbm, fibres_hbm, code_hbm, rows_hbm, readers_hbm, cell_hbm,
    out, recv_out, tensor_out, arrived_out,
    first, second, third, grads, send, recv, side, edge, corner,
    flow, fibres, code, rows, readers, cell, split, pieces, arrived, slots, slots_smem,
    onehot, table, tensor,
    load_sem, small_sem, slot_sem, out_sem, halo_send, halo_recv, fib_send, fib_recv,
    corner_send, corner_recv, row_send, row_recv, row_own, last_sem, known,
):
    nx, nz = sizes
    count = nx * nz
    ix, iz = lax.axis_index("gx"), lax.axis_index("gz")
    me = ix * nz + iz

    def at(dx, dz):
        return (lax.rem(ix + dx + nx, nx), lax.rem(iz + dz + nz, nz))

    around = [(dx, dz) for dx in (-1, 0, 1) for dz in (-1, 0, 1) if (dx, dz) != (0, 0)]

    def greet(semaphore, reach):
        there = {((dx * reach) % nx, (dz * reach) % nz) for dx, dz in around} - {(0, 0)}
        for dx, dz in sorted(there):
            pl.semaphore_signal(semaphore, inc=1, device_id=at(dx, dz), device_id_type=MESH)
        return len(there)

    barrier = pltpu.get_barrier_semaphore()
    greeted = greet(barrier, 1)

    loads = [
        pltpu.make_async_copy(velocity.at[c], first.at[c, 3:19, 0:64], load_sem.at[c]) for c in range(3)
    ]
    small = [
        pltpu.make_async_copy(src, dst, small_sem.at[i])
        for i, (src, dst) in enumerate((
            (rows_hbm, rows), (readers_hbm, readers), (code_hbm, code), (fibres_hbm, fibres), (flow_hbm, flow),
            (cell_hbm, cell),
        ))
    ]
    for copy in small + loads:
        copy.start()
    pl.semaphore_wait(barrier, greeted)

    def remote(src, dst, send_sem, recv_sem, dx, dz):
        copy = pltpu.make_async_remote_copy(
            src, dst, send_sem, recv_sem, device_id=at(dx, dz), device_id_type=MESH
        )
        copy.start()
        return copy

    def send_halo(c):
        faces = (
            (velocity.at[c, 13:16], first.at[c, 0:3, 0:64], 0, 1),
            (velocity.at[c, 0:3], first.at[c, 19:22, 0:64], 0, -1),
            (velocity.at[c, :, 56:64], side.at[c, 0], 1, 0),
            (velocity.at[c, :, 0:8], side.at[c, 1], -1, 0),
        )
        return [
            remote(src, dst, halo_send.at[4 * c + i], halo_recv.at[4 * c + i], dx, dz)
            for i, (src, dst, dx, dz) in enumerate(faces)
        ]

    halos = [send_halo(0)]
    small[0].wait()
    small[1].wait()
    slots[...] = slot_list(rows, readers)
    to_scalars = pltpu.make_async_copy(slots, slots_smem, slot_sem)
    to_scalars.start()
    greeted = greet(known.at[0], 1)

    for copy in loads:
        copy.wait()
    diagonal = [(1, 1), (-1, 1), (1, -1), (-1, -1)]
    corners = []
    for i, (dx, dz) in enumerate(diagonal):
        near, far = (18, 17) if dz == 1 else (3, 4)
        x1, x2 = (63, 62) if dx == 1 else (0, 1)
        for c in range(3):
            for r, (z, x) in enumerate(((near, x1), (near, x2), (far, x1))):
                edge[i, 3 * c + r] = first[c, z, x : x + 1, :]
        corners.append(remote(edge.at[i], corner.at[i], corner_send.at[i], corner_recv.at[i], dx, dz))

    pl.semaphore_wait(known.at[0], greeted)
    greeted = greet(known.at[1], 2)
    small[2].wait()
    small[3].wait()
    pack_fibres(fibres, code, split, pieces, arrived)
    moved = []
    for j, (dx, dz) in enumerate(around):
        off = code_offset((dx + 1) * 3 + dz + 1)
        moved.append(
            remote(pieces.at[j], arrived.at[:, off : off + CAP], fib_send.at[j], fib_recv.at[j], dx, dz)
        )
    halos.append(send_halo(1))
    pl.semaphore_wait(known.at[1], greeted)
    greeted = greet(known.at[2], 4)
    small[5].wait()
    width = 512

    @pl.loop(0, SLOT_DEV // width)
    def _(n):
        base = pl.multiple_of(n * width, width)
        onehot[:, pl.ds(base, width)] = row_onehot(cell[:, pl.ds(base, width)], count)

    small[4].wait()
    to_scalars.wait()
    ahead = DIFFUSION - 0.5 * ADVECTION * flow[...]
    behind = DIFFUSION + 0.5 * ADVECTION * flow[...]
    sub = iota((1, 8, NY), 1) < 4
    grads[:, ROWS : ROWS + 8, :] = jnp.zeros((3, 8, 128), F32)
    outs, owns = [], []
    for c in range(3):
        for copy in halos[c]:
            copy.wait_recv()
        if c == 0:
            halos.append(send_halo(2))
            for copy in corners:
                copy.wait_recv()
        here, done = first.at[c], third.at[c]
        here[3:19, 64:72, :] = jnp.where(sub, side[c, 1], side[c, 0])
        for i, (dx, dz) in enumerate(diagonal):
            near, far = (2, 1) if dz == 1 else (19, 20)
            x1, x2 = (71, 70) if dx == 1 else (64, 65)
            for r, (z, x) in enumerate(((near, x1), (near, x2), (far, x1))):
                here[z, x : x + 1, :] = corner[i, 3 * c + r]
        advance(here, second, 20, ahead, behind, 5)
        advance(second, done, 18, ahead, behind, 6)
        copy = pltpu.make_async_copy(done.at[1:17, 0:64], out.at[c], out_sem.at[c])
        copy.start()
        outs.append(copy)

        @pl.loop(0, CZ, unroll=4)
        def _(z):
            xp, xm, yp, ym = beside(done[z + 1])
            along_z = done[z + 2] - done[z]
            for j, d in enumerate((xp - xm, yp - ym, along_z)):
                d = 0.5 * d
                for h in range(2):
                    base = pl.multiple_of((z * 2 + h) * CX, CX)
                    grads[j, pl.ds(base, CX), :] = d[0:64, h * 128 : h * 128 + 128]

        @pl.loop(0, count, unroll=4)
        def _(t):
            for k in range(RCAP):
                row = slots_smem[0, RCAP * t + k]
                for j in range(3):
                    send[c, t, 3 * k + j : 3 * k + j + 1, :] = grads[j, pl.ds(row, 1), :]

        if c == 0:
            pl.semaphore_wait(known.at[2], greeted)
        own = pltpu.make_async_copy(send.at[c, me, 0:6], recv.at[c, me, 0:6], row_own.at[c])
        own.start()
        owns.append(own)

        @pl.loop(1, count)
        def _(i):
            reader = lax.rem(me + i * (2 * lax.rem(me * 37, count // 2) + 1), count)
            pltpu.make_async_remote_copy(
                send.at[c, reader, 0:6], recv.at[c, me, 0:6], row_send.at[c], row_recv.at[c],
                device_id=place(reader, nz), device_id_type=MESH,
            ).start()

    for copy in moved:
        copy.wait()
    last = [pltpu.make_async_copy(arrived, arrived_out, last_sem.at[0])]
    last[0].start()
    every = pl.ds(0, count - 1)
    for c in range(3):
        pltpu.make_async_copy(recv.at[c, every, 0:6], recv.at[c, every, 0:6], row_recv.at[c]).wait()
        owns[c].wait()
        if c < 2:
            fill_table(recv.at[c], table)
            width = 1024

            @pl.loop(0, SLOT_DEV // width)
            def _(n):
                part = pl.ds(pl.multiple_of(n * width, width), width)
                for j, row in enumerate(pick(table, onehot[:, part], cell[:, part])):
                    tensor[3 * c + j : 3 * c + j + 1, part] = row

    last.append(pltpu.make_async_copy(recv.at[2], recv_out, last_sem.at[1]))
    last.append(pltpu.make_async_copy(tensor, tensor_out, last_sem.at[2]))
    last[1].start()
    last[2].start()
    for c in range(3):
        pltpu.make_async_copy(send.at[c, every, 0:6], send.at[c, every, 0:6], row_send.at[c]).wait()
        outs[c].wait()
        for copy in halos[c]:
            copy.wait_send()
    for copy in corners:
        copy.wait_send()
    for copy in last:
        copy.wait()


def row_onehot(cell, count):
    row = cell // 128
    row = (row % RCAP) * count + row // RCAP
    return (iota((RCAP * count, cell.shape[1]), 0) == row).astype(F32).astype(BF16)


def fill_table(recv, table):
    count = recv.shape[0]
    flat = recv.reshape(count * 8, 128)
    for j in range(3):
        for k in range(RCAP):
            block = jnp.transpose(flat[pl.ds(3 * k + j, count, 8), :])
            hi = block.astype(BF16)
            at = count * k
            table[128 * j : 128 * j + 128, at : at + count] = hi
            at = at + RCAP * count
            table[128 * j : 128 * j + 128, at : at + count] = (block - hi.astype(F32)).astype(BF16)


def pick(table, onehot, cell):
    rows = jnp.dot(table[...], jnp.concatenate([onehot, onehot], axis=0), preferred_element_type=F32)
    lane = iota((128, cell.shape[1]), 0) == cell % 128
    return [jnp.sum(jnp.where(lane, rows[128 * j : 128 * j + 128], 0.0), axis=0, keepdims=True) for j in range(3)]


def hbm_spec():
    return pl.BlockSpec(memory_space=pltpu.HBM)


def any_spec():
    return pl.BlockSpec(memory_space=pl.ANY)


def vmem_spec():
    return pl.BlockSpec(memory_space=pltpu.VMEM)


def flow_call(sizes, *operands):
    count = sizes[0] * sizes[1]
    dma = pltpu.SemaphoreType.DMA
    return pl.pallas_call(
        functools.partial(flow_kernel, sizes),
        out_shape=(
            jax.ShapeDtypeStruct((3, CZ, CX, NY), F32),
            jax.ShapeDtypeStruct((count, 8, 128), F32),
            jax.ShapeDtypeStruct((6, SLOT_DEV), F32),
            jax.ShapeDtypeStruct((6, SLOT_DEV), F32),
        ),
        in_specs=[hbm_spec()] * 7,
        out_specs=(hbm_spec(),) * 4,
        scratch_shapes=[
            pltpu.VMEM((3, 22, XW, NY), F32),
            pltpu.VMEM((20, XW, NY), F32),
            pltpu.VMEM((3, 18, XW, NY), F32),
            pltpu.VMEM((3, ROWS + 8, 128), F32),
            pltpu.VMEM((3, count, 8, 128), F32),
            pltpu.VMEM((3, count, 8, 128), F32),
            pltpu.VMEM((3, 2, CZ, 8, NY), F32),
            pltpu.VMEM((4, 9, 1, NY), F32),
            pltpu.VMEM((4, 9, 1, NY), F32),
            pltpu.VMEM((1, NY), F32),
            pltpu.VMEM((6, FIB_DEV), F32),
            pltpu.VMEM((32, 128), I32),
            pltpu.VMEM((1, 192), I32),
            pltpu.VMEM((1, 192), I32),
            pltpu.VMEM((1, SLOT_DEV), I32),
            pltpu.VMEM((24, FIB_DEV), F32),
            pltpu.VMEM((8, 6, CAP), F32),
            pltpu.VMEM((6, SLOT_DEV), F32),
            pltpu.VMEM((1, 256), I32),
            pltpu.SMEM((1, 256), I32),
            pltpu.VMEM((RCAP * count, SLOT_DEV), BF16),
            pltpu.VMEM((384, 2 * RCAP * count), BF16),
            pltpu.VMEM((6, SLOT_DEV), F32),
            dma((3,)), dma((6,)), dma, dma((3,)), dma((12,)), dma((12,)), dma((8,)), dma((8,)),
            dma((4,)), dma((4,)), dma((3,)), dma((3,)), dma((3,)), dma((3,)), pltpu.SemaphoreType.REGULAR((3,)),
        ],
        compiler_params=pltpu.CompilerParams(
            collective_id=0, has_side_effects=True, vmem_limit_bytes=60 * MIB
        ),
        name="flow_and_rows",
    )(*operands)


def jeffery(orient, tensor):
    along = [sum(tensor[3 * i + j] * orient[j] for j in range(3)) for i in range(3)]
    across = [sum(tensor[3 * j + i] * orient[j] for j in range(3)) for i in range(3)]
    stretch = sum(orient[i] * along[i] for i in range(3))
    turned = []
    for i in range(3):
        strain = 0.5 * (along[i] + across[i])
        rotation = 0.5 * (along[i] - across[i])
        turned.append(orient[i] + TURN_STEP * (rotation + SHAPE_FACTOR * (strain - stretch * orient[i])))
    return turned


def turn_kernel(
    recv_hbm, tensor_hbm, cell_hbm, arrived_hbm, flow, out_hbm, flow_out,
    recv, tensor, cell, arrived, out, table, held, in_sem, flow_in, flow_store, out_sem,
):
    loads = [
        pltpu.make_async_copy(src, dst, in_sem.at[i])
        for i, (src, dst) in enumerate(
            ((recv_hbm, recv), (cell_hbm, cell), (tensor_hbm, tensor), (arrived_hbm, arrived))
        )
    ]
    brings = [pltpu.make_async_copy(flow.at[c], held.at[c], flow_in.at[c]) for c in range(3)]
    stores = [pltpu.make_async_copy(held.at[c], flow_out.at[c], flow_store.at[c]) for c in range(3)]
    for copy in loads + brings:
        copy.start()
    count = recv.shape[0]
    loads[0].wait()
    fill_table(recv, table)
    for copy in loads[1:]:
        copy.wait()
    width = 1280
    ends = []
    for n in range(SLOT_DEV // width):
        part = slice(n * width, n * width + width)
        here = cell[:, part]
        rows = [tensor[i : i + 1, part] for i in range(6)] + pick(table, row_onehot(here, count), here)
        records = arrived[:, part]
        turned = jeffery([records[3 + i : 4 + i] for i in range(3)], rows)
        out[0:3, part] = records[0:3]
        for i in range(3):
            out[3 + i : 4 + i, part] = turned[i]
        ends.append(pltpu.make_async_copy(out.at[:, part], out_hbm.at[:, part], out_sem.at[n]))
        ends[-1].start()
        if n < 3:
            brings[n].wait()
            stores[n].start()
    for copy in stores + ends:
        copy.wait()


def turn_call(recv, tensor, cell, arrived, flow):
    dma = pltpu.SemaphoreType.DMA
    return pl.pallas_call(
        turn_kernel,
        out_shape=(jax.ShapeDtypeStruct((6, SLOT_DEV), F32), jax.ShapeDtypeStruct(flow.shape, F32)),
        in_specs=[hbm_spec()] * 5,
        out_specs=(hbm_spec(), hbm_spec()),
        scratch_shapes=[
            pltpu.VMEM(recv.shape, F32),
            pltpu.VMEM(tensor.shape, F32),
            pltpu.VMEM(cell.shape, I32),
            pltpu.VMEM(arrived.shape, F32),
            pltpu.VMEM((6, SLOT_DEV), F32),
            pltpu.VMEM((384, 2 * RCAP * recv.shape[0]), BF16),
            pltpu.VMEM(flow.shape, F32),
            dma((4,)), dma((3,)), dma((3,)), dma((4,)),
        ],
        compiler_params=pltpu.CompilerParams(vmem_limit_bytes=60 * MIB),
        name="gather_and_turn",
    )(recv, tensor, cell, arrived, flow)


def per_device(sizes, velocity, mean_flow, fibres, moves, grad_rows, grad_readers, fibre_cell):
    cell = fibre_cell.reshape(1, SLOT_DEV)
    flow, recv, tensor, arrived = flow_call(
        sizes, velocity, mean_flow.reshape(1, NY), fibres, moves.reshape(32, 128),
        grad_rows.reshape(1, -1), grad_readers.reshape(1, -1), cell,
    )
    out, flow = turn_call(recv, tensor, cell, arrived, flow)
    return flow, out


def solution(mesh):
    return jax.shard_map(
        functools.partial(per_device, (mesh.shape["gx"], mesh.shape["gz"])),
        mesh=mesh,
        in_specs=(
            P(None, "gz", "gx", None),
            P(),
            P(None, ("gx", "gz")),
            P(("gx", "gz"), None),
            P(("gx", "gz")),
            P(("gx", "gz"), None),
            P(("gx", "gz")),
        ),
        out_specs=(P(None, "gz", "gx", None), P(None, ("gx", "gz"))),
        check_vma=False,
    )
```
